256 devices in a mesh: dp: 64 (over x, z, core), outer: 4 (over y).
Axes of the slice: x: 4, y: 4, z: 8, core: 2. Of those that a mesh axis runs over, the one named last changes fastest.
Arguments:
- gradients: bfloat16 [64, 4, 2, 1024, 896], P('dp', 'outer'), may hold values from -48 to 48
- errors: bfloat16 [64, 4, 2, 1024, 896], P('dp', 'outer'), may hold values from -3 to 3
- old_basis: float32 [2, 896, 8], replicated, may hold values from -4 to 4
Outputs:
- new_errors: bfloat16 [64, 4, 2, 1024, 896], P('dp', 'outer')
- new_basis: float32 [2, 896, 8], replicated
The draws below stay inside these ranges and needn't reach their ends.
All inputs are finite; a program needn't handle non-finite values.
Results may differ from the reference program's by a relative error of at most 0.001.
Values sent between devices are 32-bit elements; how exact they have to be, the bound alone decides.
A program may use at most 64 MiB of HBM per device.

```python
import math
import jax
import jax.numpy as jnp
from jax import lax

ROWS = 1024
COLS = 896
RANK = 8
MATRICES = 2
REPLICAS = 256
N_DP = 64
N_OUTER = 4


def draw_gradients(key, part):
    key = jax.random.fold_in(key, 11)
    key_list = jax.random.split(key, 7)
    common_rank = 16
    falloff = 0.88
    shape_whole = (N_DP, N_OUTER, MATRICES, ROWS, COLS)
    shared_weight = 0.3
    spread = math.log(10.0)
    left_parts = jnp.clip(jax.random.normal(key_list[0], (MATRICES, ROWS, common_rank), jnp.float32), -4.0, 4.0)
    right_parts = jnp.clip(jax.random.normal(key_list[1], (MATRICES, COLS, common_rank), jnp.float32), -4.0, 4.0)
    private = jnp.clip(jax.random.normal(key_list[2], shape_whole, jnp.float32), -4.0, 4.0)
    common = jnp.zeros((MATRICES, ROWS, COLS), jnp.float32)
    energy = 0.0
    for component in range(common_rank):
        strength = falloff ** component
        common = common + strength * left_parts[:, :, component][:, :, None] * right_parts[:, :, component][:, None, :]
        energy = energy + strength * strength
    common = common / math.sqrt(energy)
    replica_scale = jnp.exp((jax.random.uniform(key_list[4], (N_DP, N_OUTER, 1, 1, 1), jnp.float32) - 0.5) * math.log(3.0))
    row_scale = jnp.exp((jax.random.uniform(key_list[5], (MATRICES, ROWS, 1), jnp.float32) - 0.5) * spread)
    col_scale = jnp.exp((jax.random.uniform(key_list[6], (MATRICES, 1, COLS), jnp.float32) - 0.5) * spread)
    values = row_scale * col_scale * (shared_weight * common + replica_scale * private)
    values = jnp.clip(values, -48.0, 48.0)
    return values.astype(jnp.bfloat16)


def level_of(rng, dims, cuts, smallest, top_value):
    loudness, own = 1.0, jax.random.fold_in(rng, 6)
    for position, blocks in cuts:
        steps = jnp.exp(jax.random.uniform(jax.random.fold_in(own, position), (blocks,), jnp.float32, smallest / len(cuts), top_value / len(cuts)))
        loudness = loudness * jnp.repeat(steps, dims[position] // blocks).reshape([-1 if axis == position else 1 for axis in range(len(dims))])
    return loudness


def bell_draw(stream_key, extent, scale, limit, cuts=(), kind=jnp.bfloat16):
    level = level_of(stream_key, extent, cuts, -0.22, 0.18) if cuts else 1.0
    entries = jax.random.normal(stream_key, extent, jnp.float32) * scale * level
    return jnp.minimum(jnp.maximum(entries, -limit), limit).astype(kind)


def setup_inputs(seed: int = 0) -> dict:
    streams_of = jax.random.split(jax.random.key(seed), 4)
    return {
        "gradients": draw_gradients(jax.random.fold_in(streams_of[3], 71), 0),
        "errors": bell_draw(streams_of[1], (N_DP, N_OUTER, MATRICES, ROWS, COLS), 0.5, 3.0, ((0, 64), (1, 4))),
        "old_basis": bell_draw(streams_of[2], (MATRICES, COLS, RANK), 1.0, 4.0, (), jnp.float32),
    }


HIGHEST = lax.Precision.HIGHEST
EPSILON = 1e-06

def orthonormal_factor(left_mean):
    gram_matrix = jnp.einsum('krs,krt->kst', left_mean, left_mean, precision=HIGHEST)
    gram_matrix = gram_matrix + EPSILON * jnp.eye(RANK, dtype=jnp.float32)
    lower_factor = jnp.linalg.cholesky(gram_matrix)
    solved = jax.vmap(lambda factor, target: jax.scipy.linalg.solve_triangular(factor, target, lower=True))(lower_factor, jnp.swapaxes(left_mean, 1, 2))
    return jnp.swapaxes(solved, 1, 2)

def reference(gradients, errors, old_basis):
    flat_grads = gradients.reshape((REPLICAS, MATRICES, ROWS, COLS))
    flat_errors = errors.reshape((REPLICAS, MATRICES, ROWS, COLS))

    def add_left(running, members):
        merged = members[0].astype(jnp.float32) + members[1].astype(jnp.float32)
        return (running + jnp.einsum('krc,kcs->krs', merged, old_basis, precision=HIGHEST), None)
    left_sum, _ = lax.scan(add_left, jnp.zeros((MATRICES, ROWS, RANK), jnp.float32), (flat_grads, flat_errors))
    left_mean = left_sum / REPLICAS
    orthonormal = orthonormal_factor(left_mean)

    def add_right(running, members):
        merged = members[0].astype(jnp.float32) + members[1].astype(jnp.float32)
        return (running + jnp.einsum('krc,krs->kcs', merged, orthonormal, precision=HIGHEST), None)
    right_sum, _ = lax.scan(add_right, jnp.zeros((MATRICES, COLS, RANK), jnp.float32), (flat_grads, flat_errors))
    new_basis = right_sum / REPLICAS
    update = jnp.einsum('krs,kcs->krc', orthonormal, new_basis, precision=HIGHEST)

    def residual_of(members):
        merged = members[0].astype(jnp.float32) + members[1].astype(jnp.float32)
        return (merged - update).astype(jnp.bfloat16)
    new_errors = lax.map(residual_of, (flat_grads, flat_errors))
    return (new_errors.reshape(gradients.shape), new_basis)
```

```python
import functools
import itertools

import jax
import jax.numpy as jnp
from jax import lax
from jax.experimental import pallas as pl
from jax.experimental.pallas import tpu as pltpu
from jax.sharding import PartitionSpec as P

MESH = pl.DeviceIdType.MESH
HIGHEST = lax.Precision.HIGHEST
EPSILON = 1e-06
NX, NY, NZ, NC = 4, 4, 8, 2
PLANE = NX * NY * NC
REPLICAS = PLANE * NZ
BLOCK = 256


def ring(d, n):
    return min(d % n, n - d % n)


PLANE_OFFSETS = sorted(
    (o for o in itertools.product(range(NX), range(NY), range(NC)) if any(o)),
    key=lambda o: -(ring(o[0], NX) + ring(o[1], NY) + 0.5 * o[2]),
)
Z_OFFSETS = sorted(range(1, NZ), key=lambda d: -ring(d, NZ))


def split3(value):
    high = value.astype(jnp.bfloat16).astype(jnp.float32)
    rest = value - high
    middle = rest.astype(jnp.bfloat16).astype(jnp.float32)
    return high, middle, rest - middle


def stacked(value):
    return jnp.concatenate(split3(value), axis=0).astype(jnp.bfloat16)


def fold(product):
    return product[0:8] + product[8:16] + product[16:24]


def reduce_kernel(
    g_hbm, e_hbm, q_hbm,
    gv, ev, factors, basis,
    qv, send1, slot1, part1, zslot1, final1, gather1,
    send2, slot2, part2, zslot2, final2, gather2,
    in_sem, q_sem, send_sem, recv_sem,
):
    matrices, rows, cols = gv.shape
    per = rows // BLOCK
    dp, y = lax.axis_index("dp"), lax.axis_index("outer")
    x, z, c = lax.div(dp, NZ * NC), lax.rem(lax.div(dp, NC), NZ), lax.rem(dp, NC)
    mine = (x * NY + y) * NC + c

    q_copy = pltpu.make_async_copy(q_hbm, qv, q_sem)
    q_copy.start()
    loads = []
    for m in range(matrices):
        for i in range(per):
            at = pl.ds(i * BLOCK, BLOCK)
            pair = []
            for a, (src, dst) in enumerate(((g_hbm, gv), (e_hbm, ev))):
                copy = pltpu.make_async_copy(src.at[m, at], dst.at[m, at], in_sem.at[m, i, a])
                copy.start()
                pair.append(copy)
            loads.append((m, i, pair))

    plane = []
    for dx, dy, dc in PLANE_OFFSETS:
        tx, ty, tc = lax.rem(x + dx, NX), lax.rem(y + dy, NY), lax.rem(c + dc, NC)
        plane.append(((tx * NY + ty) * NC + tc, {"dp": (tx * NZ + z) * NC + tc, "outer": ty}))
    column = [{"dp": (x * NZ + lax.rem(z + d, NZ)) * NC + c, "outer": y} for d in Z_OFFSETS]
    barrier = pltpu.get_barrier_semaphore()
    for device in [d for _, d in plane] + column:
        pl.semaphore_signal(barrier, inc=1, device_id=device, device_id_type=MESH)

    def wait_all(ref, sem):
        pltpu.make_async_copy(ref, ref, sem).wait()

    def remote(src, dst, k, device):
        pltpu.make_async_remote_copy(
            src_ref=src, dst_ref=dst, send_sem=send_sem.at[k], recv_sem=recv_sem.at[k],
            device_id=device, device_id_type=MESH,
        ).start()

    def scatter(send, slot, k):
        for index, device in plane:
            remote(send.at[index], slot.at[mine], k, device)
        pltpu.make_async_copy(send.at[mine], slot.at[mine], recv_sem.at[k]).start()

    def exchange(slot, part, zslot, k):
        wait_all(slot, recv_sem.at[k])
        total = slot[0]
        for i in range(1, PLANE):
            total = total + slot[i]
        part[...] = total
        for device in column:
            remote(part, zslot.at[z], k + 1, device)
        pltpu.make_async_copy(part, zslot.at[z], recv_sem.at[k + 1]).start()

    def spread(zslot, final, gather, k):
        wait_all(zslot, recv_sem.at[k + 1])
        total = zslot[0]
        for i in range(1, NZ):
            total = total + zslot[i]
        final[...] = total * (1.0 / REPLICAS)
        for _, device in plane:
            remote(final, gather.at[mine], k + 2, device)
        pltpu.make_async_copy(final, gather.at[mine], recv_sem.at[k + 2]).start()

    def assembled(gather, m, blocks):
        tiles = [
            jnp.concatenate([gather[m * 16 + b], gather[m * 16 + 8 + b]], axis=0) for b in range(blocks)
        ]
        return jnp.concatenate(tiles, axis=1)

    def place(send, m, b, tile):
        send[m * 16 + b] = tile[0:4]
        send[m * 16 + 8 + b] = tile[4:8]

    q_copy.wait()
    q_terms = [stacked(qv[m]) for m in range(matrices)]
    contract_last = (((1,), (1,)), ((), ()))
    for m, i, pair in loads:
        for copy in pair:
            copy.wait()
        at = pl.ds(i * BLOCK, BLOCK)
        left = fold(
            lax.dot_general(q_terms[m], gv[m, at], contract_last, preferred_element_type=jnp.float32)
            + lax.dot_general(q_terms[m], ev[m, at], contract_last, preferred_element_type=jnp.float32)
        )
        for b in range(BLOCK // 128):
            place(send1, m, i * (BLOCK // 128) + b, left[:, b * 128 : (b + 1) * 128])

    pl.semaphore_wait(barrier, len(plane) + len(column))
    scatter(send1, slot1, 0)
    exchange(slot1, part1, zslot1, 0)
    spread(zslot1, final1, gather1, 0)
    wait_all(gather1, recv_sem.at[2])

    left_mean = [assembled(gather1, m, rows // 128) for m in range(matrices)]
    for m in range(matrices):
        terms = stacked(left_mean[m])
        right = fold(
            jnp.dot(terms, gv[m], preferred_element_type=jnp.float32)
            + jnp.dot(terms, ev[m], preferred_element_type=jnp.float32)
        )
        for b in range(cols // 128):
            place(send2, m, b, right[:, b * 128 : (b + 1) * 128])
        for b in range(cols // 128, 8):
            place(send2, m, b, jnp.zeros((8, 128), jnp.float32))
    scatter(send2, slot2, 3)

    row_of = lax.broadcasted_iota(jnp.int32, (8, 1), 0)
    eye = (
        lax.broadcasted_iota(jnp.int32, (8, 8), 0) == lax.broadcasted_iota(jnp.int32, (8, 8), 1)
    ).astype(jnp.float32)
    inverses = []
    for m in range(matrices):
        gram = lax.dot_general(
            left_mean[m], left_mean[m], contract_last, precision=HIGHEST, preferred_element_type=jnp.float32
        )
        gram = gram + EPSILON * eye
        inverse, solved = eye, left_mean[m]
        for k in range(8):
            pivot = jnp.sqrt(gram[k : k + 1, k : k + 1])
            across = gram[k : k + 1, :] / pivot
            below = jnp.where(row_of > k, gram[:, k : k + 1] / pivot, 0.0)
            gram = gram - below * across
            first = inverse[k : k + 1, :] / pivot
            inverse = jnp.where(row_of == k, first, inverse - below * first)
            first = solved[k : k + 1, :] / pivot
            solved = jnp.where(row_of == k, first, solved - below * first)
        inverses.append(inverse)
        o1, o2, o3 = split3(solved)
        wide = jnp.concatenate([o1, o1, o2, o2, o1, o3, jnp.zeros((80, rows), jnp.float32)], axis=0)
        factors[m] = jnp.transpose(wide).astype(jnp.bfloat16)

    exchange(slot2, part2, zslot2, 3)
    spread(zslot2, final2, gather2, 3)
    wait_all(gather2, recv_sem.at[5])
    for m in range(matrices):
        raw = assembled(gather2, m, cols // 128)
        total = inverses[m][:, 0:1] * raw[0:1, :]
        for t in range(1, 8):
            total = total + inverses[m][:, t : t + 1] * raw[t : t + 1, :]
        basis[m] = total

    for k in (0, 3):
        wait_all(slot1.at[pl.ds(0, PLANE - 1)], send_sem.at[k])
        wait_all(zslot1.at[pl.ds(0, NZ - 1)], send_sem.at[k + 1])
        wait_all(gather1.at[pl.ds(0, PLANE - 1)], send_sem.at[k + 2])


def residual_kernel(gv, ev, factors, basis, out_hbm, basis_hbm, buffer, out_sem, basis_sem):
    matrices, rows, cols = gv.shape
    basis_copy = pltpu.make_async_copy(basis, basis_hbm, basis_sem)
    basis_copy.start()
    for m in range(matrices):
        b1, b2, b3 = split3(basis[m])
        terms = jnp.concatenate(
            [b1, b2, b1, b2, b3, b1, jnp.zeros((80, cols), jnp.float32)], axis=0
        ).astype(jnp.bfloat16)
        for i in range(rows // BLOCK):
            at = pl.ds(i * BLOCK, BLOCK)
            update = jnp.dot(factors[m, at], terms, preferred_element_type=jnp.float32)
            merged = gv[m, at].astype(jnp.float32) + ev[m, at].astype(jnp.float32)
            buffer[m, at] = (merged - update).astype(jnp.bfloat16)
            pltpu.make_async_copy(buffer.at[m, at], out_hbm.at[m, at], out_sem).start()
    pltpu.make_async_copy(buffer, out_hbm, out_sem).wait()
    basis_copy.wait()


def shards(gradients, errors, old_basis):
    _, _, matrices, rows, cols = gradients.shape
    rank = old_basis.shape[2]
    any_space = pl.BlockSpec(memory_space=pl.ANY)
    vmem = pl.BlockSpec(memory_space=pltpu.VMEM)
    f32 = jnp.float32
    stage = [
        pltpu.VMEM((PLANE, 4, 128), f32),
        pltpu.VMEM((PLANE, 4, 128), f32),
        pltpu.VMEM((4, 128), f32),
        pltpu.VMEM((NZ, 4, 128), f32),
        pltpu.VMEM((4, 128), f32),
        pltpu.VMEM((PLANE, 4, 128), f32),
    ]
    gv, ev, factors, basis = pl.pallas_call(
        reduce_kernel,
        out_shape=(
            pltpu.VMEM((matrices, rows, cols), jnp.bfloat16),
            pltpu.VMEM((matrices, rows, cols), jnp.bfloat16),
            pltpu.VMEM((matrices, rows, 128), jnp.bfloat16),
            pltpu.VMEM((matrices, rank, cols), f32),
        ),
        in_specs=[pl.BlockSpec(memory_space=pltpu.HBM)] * 3,
        out_specs=(vmem,) * 4,
        scratch_shapes=[pltpu.VMEM((matrices, rank, cols), f32)]
        + stage
        + stage
        + [
            pltpu.SemaphoreType.DMA((matrices, rows // BLOCK, 2)),
            pltpu.SemaphoreType.DMA,
            pltpu.SemaphoreType.DMA((6,)),
            pltpu.SemaphoreType.DMA((6,)),
        ],
        compiler_params=pltpu.CompilerParams(
            collective_id=0, has_side_effects=True, vmem_limit_bytes=24 << 20
        ),
        name="reduce",
    )(gradients[0, 0], errors[0, 0], jnp.swapaxes(old_basis, 1, 2))
    residual, new_basis = pl.pallas_call(
        residual_kernel,
        out_shape=(
            jax.ShapeDtypeStruct((matrices, rows, cols), jnp.bfloat16),
            jax.ShapeDtypeStruct((matrices, rank, cols), f32),
        ),
        in_specs=[vmem] * 4,
        out_specs=(any_space,) * 2,
        scratch_shapes=[
            pltpu.VMEM((matrices, rows, cols), jnp.bfloat16),
            pltpu.SemaphoreType.DMA,
            pltpu.SemaphoreType.DMA,
        ],
        compiler_params=pltpu.CompilerParams(vmem_limit_bytes=24 << 20),
        name="residual",
    )(gv, ev, factors, basis)
    return residual[None, None], jnp.swapaxes(new_basis, 1, 2)


def solution(mesh):
    in_specs = (P("dp", "outer", None, None, None), P("dp", "outer", None, None, None), P())
    out_specs = (P("dp", "outer", None, None, None), P())
    return jax.shard_map(shards, mesh=mesh, in_specs=in_specs, out_specs=out_specs, check_vma=False)
```

```python
import functools
import itertools

import jax
import jax.numpy as jnp
from jax import lax
from jax.experimental import pallas as pl
from jax.experimental.pallas import tpu as pltpu
from jax.sharding import PartitionSpec as P

MESH = pl.DeviceIdType.MESH
HIGHEST = lax.Precision.HIGHEST
EPSILON = 1e-06
NX, NY, NZ, NC = 4, 4, 8, 2
PLANE = NX * NY * NC
REPLICAS = PLANE * NZ
BLOCK = 256
LOAD = 512
FAR = 5


def ring(d, n):
    return min(d % n, n - d % n)


XY_OFFSETS = sorted(itertools.product(range(NX), range(NY)), key=lambda o: -(ring(o[0], NX) + ring(o[1], NY)))
Z_OFFSETS = sorted(range(1, NZ), key=lambda d: -ring(d, NZ))


def split3(value):
    high = value.astype(jnp.bfloat16).astype(jnp.float32)
    rest = value - high
    middle = rest.astype(jnp.bfloat16).astype(jnp.float32)
    return high, middle, rest - middle


def stacked(value):
    return jnp.concatenate(split3(value), axis=0).astype(jnp.bfloat16)


def tree_sum(terms):
    while len(terms) > 1:
        terms = [a + b for a, b in zip(terms[::2], terms[1::2])]
    return terms[0]


def fold(product):
    return product[0:8] + product[8:16] + product[16:24]


def reduce_kernel(
    g_hbm, e_hbm, q_hbm,
    merged, factors, basis,
    gv, ev, qv, send1, slot1, part1, zslot1, final1, gather1,
    send2, slot2, part2, zslot2, final2, gather2,
    in_sem, q_sem, send_sem, recv_sem,
):
    _, rows, cols = gv.shape
    per = rows // LOAD
    dp, y = lax.axis_index("dp"), lax.axis_index("outer")
    x, z, c = lax.div(dp, NZ * NC), lax.rem(lax.div(dp, NC), NZ), lax.rem(dp, NC)
    own, other = c, 1 - c
    place_xy = x * NY + y
    sender = place_xy * NC + c

    here, across = [], []
    for dx, dy in XY_OFFSETS:
        tx, ty = lax.rem(x + dx, NX), lax.rem(y + dy, NY)
        index = tx * NY + ty
        if dx or dy:
            here.append((index, {"dp": (tx * NZ + z) * NC + own, "outer": ty}))
        across.append((index, {"dp": (tx * NZ + z) * NC + other, "outer": ty}))
    column = [{"dp": (x * NZ + lax.rem(z + d, NZ)) * NC + c, "outer": y} for d in Z_OFFSETS]
    partners = [d for _, d in across[:4]] + column[:3] + [d for _, d in here + across[4:]] + column[3:]
    barrier = pltpu.get_barrier_semaphore()
    for device in partners:
        pl.semaphore_signal(barrier, inc=1, device_id=device, device_id_type=MESH)

    q_copy = pltpu.make_async_copy(q_hbm, qv, q_sem)
    q_copy.start()
    loads = []
    for n, m in enumerate((other, own)):
        for i in range(per):
            at = pl.ds(i * LOAD, LOAD)
            pair = []
            for a, (src, dst) in enumerate(((g_hbm, gv), (e_hbm, ev))):
                copy = pltpu.make_async_copy(src.at[m, at], dst.at[m, at], in_sem.at[n, i, a])
                copy.start(priority=n)
                pair.append(copy)
            loads.append((n, m, i, pair))

    def wait_all(ref, sem):
        pltpu.make_async_copy(ref, ref, sem).wait()

    def remote(src, dst, send, recv, device):
        pltpu.make_async_remote_copy(
            src_ref=src, dst_ref=dst, send_sem=send_sem.at[send], recv_sem=recv_sem.at[recv],
            device_id=device, device_id_type=MESH,
        ).start()

    def scatter_across(send, m, slot, k):
        for index, device in across:
            remote(send.at[m, index], slot.at[sender], k, k, device)

    def scatter_here(send, m, slot, k):
        for index, device in here:
            remote(send.at[m, index], slot.at[sender], k, k, device)
        pltpu.make_async_copy(send.at[m, place_xy], slot.at[sender], recv_sem.at[k]).start()

    def exchange(slot, part, zslot, k):
        wait_all(slot, recv_sem.at[k])
        part[...] = tree_sum([slot[i] for i in range(PLANE)])
        for device in column:
            remote(part, zslot.at[z], k + 1, k + 1, device)
        pltpu.make_async_copy(part, zslot.at[z], recv_sem.at[k + 1]).start()

    def spread(zslot, final, gather, m, k):
        wait_all(zslot, recv_sem.at[k + 1])
        final[...] = tree_sum([zslot[i] for i in range(NZ)]) * (1.0 / REPLICAS)
        for _, device in here[:FAR]:
            remote(final, gather.at[m, place_xy], k + 2, k + 2, device)
        for _, device in across:
            remote(final, gather.at[m, place_xy], k + 2, k + 3, device)
        for _, device in here[FAR:]:
            remote(final, gather.at[m, place_xy], k + 2, k + 2, device)
        pltpu.make_async_copy(final, gather.at[m, place_xy], recv_sem.at[k + 2]).start()

    def assembled(gather, m, blocks):
        tiles = [jnp.concatenate([gather[m, b], gather[m, 8 + b]], axis=0) for b in range(blocks)]
        return jnp.concatenate(tiles, axis=1)

    def place(send, m, b, tile):
        send[m, b] = tile[0:4]
        send[m, 8 + b] = tile[4:8]

    contract_last = (((1,), (1,)), ((), ()))
    q_copy.wait()
    q_terms = [stacked(qv[m]) for m in (other, own)]
    for n, m, i, pair in loads:
        for copy in pair:
            copy.wait()
        at = pl.ds(i * LOAD, LOAD)
        left = fold(
            lax.dot_general(q_terms[n], gv[m, at], contract_last, preferred_element_type=jnp.float32)
            + lax.dot_general(q_terms[n], ev[m, at], contract_last, preferred_element_type=jnp.float32)
        )
        for b in range(LOAD // 128):
            place(send1, m, i * (LOAD // 128) + b, left[:, b * 128 : (b + 1) * 128])
        if n == 1 and i == per - 2:
            pl.semaphore_wait(barrier, len(partners))
            scatter_across(send1, other, slot1, 0)
    scatter_here(send1, own, slot1, 0)
    for n in range(2):
        for i in range(rows // BLOCK):
            at = pl.ds(i * BLOCK, BLOCK)
            merged[n, at] = gv[n, at].astype(jnp.float32) + ev[n, at].astype(jnp.float32)
    exchange(slot1, part1, zslot1, 0)
    spread(zslot1, final1, gather1, own, 0)

    def right(m):
        mean = assembled(gather1, m, rows // 128)
        terms = stacked(mean)
        product = fold(
            jnp.dot(terms, gv[m], preferred_element_type=jnp.float32)
            + jnp.dot(terms, ev[m], preferred_element_type=jnp.float32)
        )
        for b in range(cols // 128):
            place(send2, m, b, product[:, b * 128 : (b + 1) * 128])
        for b in range(cols // 128, 8):
            place(send2, m, b, jnp.zeros((8, 128), jnp.float32))
        return mean

    wait_all(gather1.at[own], recv_sem.at[2])
    mean_own = right(own)
    scatter_across(send2, own, slot2, 4)
    wait_all(gather1.at[other], recv_sem.at[3])
    mean_other = right(other)
    scatter_here(send2, other, slot2, 4)

    row_of = lax.broadcasted_iota(jnp.int32, (8, 1), 0)
    eye = (
        lax.broadcasted_iota(jnp.int32, (8, 8), 0) == lax.broadcasted_iota(jnp.int32, (8, 8), 1)
    ).astype(jnp.float32)
    inverses = []
    for m, mean in ((own, mean_own), (other, mean_other)):
        gram = lax.dot_general(mean, mean, contract_last, precision=HIGHEST, preferred_element_type=jnp.float32)
        gram = gram + EPSILON * eye
        inverse, solved = eye, mean
        for k in range(8):
            pivot = jnp.sqrt(gram[k : k + 1, k : k + 1])
            across_row = gram[k : k + 1, :] / pivot
            below = jnp.where(row_of > k, gram[:, k : k + 1] / pivot, 0.0)
            gram = gram - below * across_row
            first = inverse[k : k + 1, :] / pivot
            inverse = jnp.where(row_of == k, first, inverse - below * first)
            first = solved[k : k + 1, :] / pivot
            solved = jnp.where(row_of == k, first, solved - below * first)
        inverses.append((m, inverse))
        o1, o2, o3 = split3(solved)
        wide = jnp.concatenate([o1, o1, o2, o2, o1, o3, jnp.zeros((80, rows), jnp.float32)], axis=0)
        factors[m] = jnp.transpose(wide).astype(jnp.bfloat16)

    exchange(slot2, part2, zslot2, 4)
    spread(zslot2, final2, gather2, other, 4)
    wait_all(gather2.at[other], recv_sem.at[6])
    wait_all(gather2.at[own], recv_sem.at[7])
    for m, inverse in inverses:
        raw = assembled(gather2, m, cols // 128)
        basis[m] = tree_sum([inverse[:, t : t + 1] * raw[t : t + 1, :] for t in range(8)])

    for k in (0, 4):
        wait_all(slot1.at[pl.ds(0, PLANE - 1)], send_sem.at[k])
        wait_all(zslot1.at[pl.ds(0, NZ - 1)], send_sem.at[k + 1])
        wait_all(slot1.at[pl.ds(0, PLANE - 1)], send_sem.at[k + 2])


def residual_kernel(merged, factors, basis, out_hbm, basis_hbm, buffer, out_sem, basis_sem):
    matrices, rows, cols = merged.shape
    basis_copy = pltpu.make_async_copy(basis, basis_hbm, basis_sem)
    basis_copy.start()
    for m in range(matrices):
        b1, b2, b3 = split3(basis[m])
        terms = jnp.concatenate(
            [b1, b2, b1, b2, b3, b1, jnp.zeros((80, cols), jnp.float32)], axis=0
        ).astype(jnp.bfloat16)
        for i in range(rows // BLOCK):
            at = pl.ds(i * BLOCK, BLOCK)
            update = jnp.dot(factors[m, at], terms, preferred_element_type=jnp.float32)
            buffer[m, at] = (merged[m, at] - update).astype(jnp.bfloat16)
            pltpu.make_async_copy(buffer.at[m, at], out_hbm.at[m, at], out_sem).start()
    pltpu.make_async_copy(buffer, out_hbm, out_sem).wait()
    basis_copy.wait()


def shards(gradients, errors, old_basis):
    _, _, matrices, rows, cols = gradients.shape
    rank = old_basis.shape[2]
    any_space = pl.BlockSpec(memory_space=pl.ANY)
    vmem = pl.BlockSpec(memory_space=pltpu.VMEM)
    f32 = jnp.float32
    stage = [
        pltpu.VMEM((matrices, 16, 4, 128), f32),
        pltpu.VMEM((PLANE, 4, 128), f32),
        pltpu.VMEM((4, 128), f32),
        pltpu.VMEM((NZ, 4, 128), f32),
        pltpu.VMEM((4, 128), f32),
        pltpu.VMEM((matrices, 16, 4, 128), f32),
    ]
    merged, factors, basis = pl.pallas_call(
        reduce_kernel,
        out_shape=(
            pltpu.VMEM((matrices, rows, cols), f32),
            pltpu.VMEM((matrices, rows, 128), jnp.bfloat16),
            pltpu.VMEM((matrices, rank, cols), f32),
        ),
        in_specs=[pl.BlockSpec(memory_space=pltpu.HBM)] * 3,
        out_specs=(vmem,) * 3,
        scratch_shapes=[
            pltpu.VMEM((matrices, rows, cols), jnp.bfloat16),
            pltpu.VMEM((matrices, rows, cols), jnp.bfloat16),
            pltpu.VMEM((matrices, rank, cols), f32),
        ]
        + stage
        + stage
        + [
            pltpu.SemaphoreType.DMA((matrices, rows // LOAD, 2)),
            pltpu.SemaphoreType.DMA,
            pltpu.SemaphoreType.DMA((8,)),
            pltpu.SemaphoreType.DMA((8,)),
        ],
        compiler_params=pltpu.CompilerParams(
            collective_id=0, has_side_effects=True, vmem_limit_bytes=50 << 20
        ),
        name="reduce",
    )(gradients[0, 0], errors[0, 0], jnp.swapaxes(old_basis, 1, 2))
    residual, new_basis = pl.pallas_call(
        residual_kernel,
        out_shape=(
            jax.ShapeDtypeStruct((matrices, rows, cols), jnp.bfloat16),
            jax.ShapeDtypeStruct((matrices, rank, cols), f32),
        ),
        in_specs=[vmem] * 3,
        out_specs=(any_space,) * 2,
        scratch_shapes=[
            pltpu.VMEM((matrices, rows, cols), jnp.bfloat16),
            pltpu.SemaphoreType.DMA,
            pltpu.SemaphoreType.DMA,
        ],
        compiler_params=pltpu.CompilerParams(vmem_limit_bytes=24 << 20),
        name="residual",
    )(merged, factors, basis)
    return residual[None, None], jnp.swapaxes(new_basis, 1, 2)


def solution(mesh):
    in_specs = (P("dp", "outer", None, None, None), P("dp", "outer", None, None, None), P())
    out_specs = (P("dp", "outer", None, None, None), P())
    return jax.shard_map(shards, mesh=mesh, in_specs=in_specs, out_specs=out_specs, check_vma=False)
```

```python
import functools
import itertools

import jax
import jax.numpy as jnp
from jax import lax
from jax.experimental import pallas as pl
from jax.experimental.pallas import tpu as pltpu
from jax.sharding import PartitionSpec as P

MESH = pl.DeviceIdType.MESH
HIGHEST = lax.Precision.HIGHEST
EPSILON = 1e-06
NX, NY, NZ, NC = 4, 4, 8, 2
PLANE = NX * NY * NC
REPLICAS = PLANE * NZ
BLOCK = 256
LOAD = 512
FAR = 5
HALF, FIRST, SECOND = 2, 2, 0


def ring(d, n):
    return min(d % n, n - d % n)


XY_OFFSETS = sorted(itertools.product(range(NX), range(NY)), key=lambda o: -(ring(o[0], NX) + ring(o[1], NY)))
Z_OFFSETS = sorted(range(1, NZ), key=lambda d: -ring(d, NZ))


def split3(value):
    high = value.astype(jnp.bfloat16).astype(jnp.float32)
    rest = value - high
    middle = rest.astype(jnp.bfloat16).astype(jnp.float32)
    return high, middle, rest - middle


def stacked(value):
    return jnp.concatenate(split3(value), axis=0).astype(jnp.bfloat16)


def tree_sum(terms):
    while len(terms) > 1:
        terms = [a + b for a, b in zip(terms[::2], terms[1::2])]
    return terms[0]


def fold(product):
    return product[0:8] + product[8:16] + product[16:24]


def reduce_kernel(
    g_hbm, e_hbm, q_hbm,
    merged, factors, basis,
    gv, ev, qv, send1, slot1, part1, zslot1, final1, gather1,
    send2, slot2, part2, zslot2, final2, gather2,
    in_sem, q_sem, send_sem, recv_sem,
):
    _, rows, cols = gv.shape
    per = rows // LOAD
    dp, y = lax.axis_index("dp"), lax.axis_index("outer")
    x, z, c = lax.div(dp, NZ * NC), lax.rem(lax.div(dp, NC), NZ), lax.rem(dp, NC)
    own, other = c, 1 - c
    sender = (x * NY + y) * NC + c
    half, column_of_half = lax.div(x, HALF), lax.rem(x, HALF)
    mine = column_of_half * NY + y

    q_copy = pltpu.make_async_copy(q_hbm, qv, q_sem)
    q_copy.start()
    loads = []
    for n, m in enumerate((other, own)):
        for i in range(per):
            at = pl.ds(i * LOAD, LOAD)
            pair = []
            for a, (src, dst) in enumerate(((g_hbm, gv), (e_hbm, ev))):
                copy = pltpu.make_async_copy(src.at[m, at], dst.at[m, at], in_sem.at[n, i, a])
                copy.start(priority=1)
                pair.append(copy)
            loads.append((n, m, i, pair))

    here, across = [], []
    for dx, dy in XY_OFFSETS:
        tx, ty = lax.rem(x + dx, NX), lax.rem(y + dy, NY)
        if dx or dy:
            here.append({"dp": (tx * NZ + z) * NC + own, "outer": ty})
        across.append({"dp": (tx * NZ + z) * NC + other, "outer": ty})
    column = [{"dp": (x * NZ + lax.rem(z + d, NZ)) * NC + c, "outer": y} for d in Z_OFFSETS]
    partners = across[:4] + column[:3] + here + across[4:] + column[3:]
    barrier = pltpu.get_barrier_semaphore()
    for device in partners:
        pl.semaphore_signal(barrier, inc=1, device_id=device, device_id_type=MESH)

    def wait_all(ref, sem):
        pltpu.make_async_copy(ref, ref, sem).wait()

    def remote(src, dst, send, recv, device):
        pltpu.make_async_remote_copy(
            src_ref=src, dst_ref=dst, send_sem=send_sem.at[send], recv_sem=recv_sem.at[recv],
            device_id=device, device_id_type=MESH,
        ).start()

    def targets(core, first):
        for dy in (2, 1, 3, 0):
            for i in range(HALF):
                ty = lax.rem(y + dy, NY)
                yield dy, i, i * NY + ty, {"dp": ((first + i) * NZ + z) * NC + core, "outer": ty}

    def scatter_across(send, m, slot, k, first):
        for _, _, index, device in targets(other, first):
            remote(send.at[m, index], slot.at[sender], k, k, device)

    def scatter_here(send, m, slot, k, first):
        for dy, i, index, device in targets(own, first):
            if dy:
                remote(send.at[m, index], slot.at[sender], k, k, device)
                continue

            @pl.when(x == first + i)
            def _():
                pltpu.make_async_copy(send.at[m, index], slot.at[sender], recv_sem.at[k]).start()

            @pl.when(x != first + i)
            def _():
                remote(send.at[m, index], slot.at[sender], k, k, device)

    def exchange(slot, part, zslot, k):
        wait_all(slot, recv_sem.at[k])
        part[...] = tree_sum([slot[i] for i in range(PLANE)])
        for device in column:
            remote(part, zslot.at[z], k + 1, k + 1, device)
        pltpu.make_async_copy(part, zslot.at[z], recv_sem.at[k + 1]).start()

    def spread(zslot, final, gather, m, k):
        wait_all(zslot, recv_sem.at[k + 1])
        final[...] = tree_sum([zslot[i] for i in range(NZ)]) * (1.0 / REPLICAS)
        for device in here[:FAR]:
            remote(final, gather.at[m, mine], k + 2, k + 2, device)
        for device in across:
            remote(final, gather.at[m, mine], k + 2, k + 3, device)
        for device in here[FAR:]:
            remote(final, gather.at[m, mine], k + 2, k + 2, device)
        pltpu.make_async_copy(final, gather.at[m, mine], recv_sem.at[k + 2]).start()

    def assembled(gather, m, blocks):
        return jnp.concatenate([gather[m, b] for b in range(blocks)], axis=1)

    def place(send, m, b, tile):
        send[m, b] = tile

    contract_last = (((1,), (1,)), ((), ()))
    q_copy.wait()
    q_terms = [stacked(qv[m]) for m in (other, own)]
    for n, m, i, pair in loads:
        for copy in pair:
            copy.wait()
        at = pl.ds(i * LOAD, LOAD)
        left = fold(
            lax.dot_general(q_terms[n], gv[m, at], contract_last, preferred_element_type=jnp.float32)
            + lax.dot_general(q_terms[n], ev[m, at], contract_last, preferred_element_type=jnp.float32)
        )
        for b in range(LOAD // 128):
            place(send1, m, i * (LOAD // 128) + b, left[:, b * 128 : (b + 1) * 128])
    pl.semaphore_wait(barrier, len(partners))
    scatter_across(send1, other, slot1, 0, FIRST)
    scatter_here(send1, own, slot1, 0, FIRST)
    for n in range(2):
        for i in range(rows // BLOCK):
            at = pl.ds(i * BLOCK, BLOCK)
            merged[n, at] = gv[n, at].astype(jnp.float32) + ev[n, at].astype(jnp.float32)

    @pl.when(half == FIRST // HALF)
    def _():
        exchange(slot1, part1, zslot1, 0)
        spread(zslot1, final1, gather1, own, 0)


    def right(m):
        mean = assembled(gather1, m, rows // 128)
        terms = stacked(mean)
        product = fold(
            jnp.dot(terms, gv[m], preferred_element_type=jnp.float32)
            + jnp.dot(terms, ev[m], preferred_element_type=jnp.float32)
        )
        for b in range(cols // 128):
            place(send2, m, b, product[:, b * 128 : (b + 1) * 128])
        for b in range(cols // 128, 8):
            place(send2, m, b, jnp.zeros((8, 128), jnp.float32))
        return mean

    wait_all(gather1.at[own], recv_sem.at[2])
    wait_all(gather1.at[other], recv_sem.at[3])
    mean_own = right(own)
    mean_other = right(other)
    scatter_across(send2, own, slot2, 4, SECOND)
    scatter_here(send2, other, slot2, 4, SECOND)

    row_of = lax.broadcasted_iota(jnp.int32, (8, 1), 0)
    eye = (
        lax.broadcasted_iota(jnp.int32, (8, 8), 0) == lax.broadcasted_iota(jnp.int32, (8, 8), 1)
    ).astype(jnp.float32)
    solutions = []
    for m, mean in ((own, mean_own), (other, mean_other)):
        gram = lax.dot_general(mean, mean, contract_last, precision=HIGHEST, preferred_element_type=jnp.float32)
        gram = gram + EPSILON * eye
        inverse, solved = eye, mean
        for k in range(8):
            pivot = jnp.sqrt(gram[k : k + 1, k : k + 1])
            across_row = gram[k : k + 1, :] / pivot
            below = jnp.where(row_of > k, gram[:, k : k + 1] / pivot, 0.0)
            gram = gram - below * across_row
            first = inverse[k : k + 1, :] / pivot
            inverse = jnp.where(row_of == k, first, inverse - below * first)
            first = solved[k : k + 1, :] / pivot
            solved = jnp.where(row_of == k, first, solved - below * first)
        solutions.append((m, inverse, solved))

    @pl.when(half == SECOND // HALF)
    def _():
        exchange(slot2, part2, zslot2, 4)

    for m, _, solved in solutions:
        o1, o2, o3 = split3(solved)
        wide = jnp.concatenate([o1, o1, o2, o2, o1, o3, jnp.zeros((80, rows), jnp.float32)], axis=0)
        factors[m] = jnp.transpose(wide).astype(jnp.bfloat16)

    @pl.when(half == SECOND // HALF)
    def _():
        spread(zslot2, final2, gather2, other, 4)

    wait_all(gather2.at[other], recv_sem.at[6])
    wait_all(gather2.at[own], recv_sem.at[7])
    for m, inverse, _ in solutions:
        raw = assembled(gather2, m, cols // 128)
        basis[m] = tree_sum([inverse[:, t : t + 1] * raw[t : t + 1, :] for t in range(8)])

    for k, first in ((0, FIRST), (4, SECOND)):

        @pl.when(half == first // HALF)
        def _():
            wait_all(slot1.at[pl.ds(0, NC * HALF * NY - 1)], send_sem.at[k])
            wait_all(zslot1.at[pl.ds(0, NZ - 1)], send_sem.at[k + 1])
            wait_all(slot1.at[pl.ds(0, PLANE - 1)], send_sem.at[k + 2])

        @pl.when(half != first // HALF)
        def _():
            wait_all(slot1.at[pl.ds(0, NC * HALF * NY)], send_sem.at[k])


def residual_kernel(merged, factors, basis, out_hbm, basis_hbm, buffer, out_sem, basis_sem):
    matrices, rows, cols = merged.shape
    basis_copy = pltpu.make_async_copy(basis, basis_hbm, basis_sem)
    basis_copy.start()
    for m in range(matrices):
        b1, b2, b3 = split3(basis[m])
        terms = jnp.concatenate(
            [b1, b2, b1, b2, b3, b1, jnp.zeros((80, cols), jnp.float32)], axis=0
        ).astype(jnp.bfloat16)
        for i in range(rows // BLOCK):
            at = pl.ds(i * BLOCK, BLOCK)
            update = jnp.dot(factors[m, at], terms, preferred_element_type=jnp.float32)
            buffer[m, at] = (merged[m, at] - update).astype(jnp.bfloat16)
            pltpu.make_async_copy(buffer.at[m, at], out_hbm.at[m, at], out_sem).start()
    pltpu.make_async_copy(buffer, out_hbm, out_sem).wait()
    basis_copy.wait()


def shards(gradients, errors, old_basis):
    _, _, matrices, rows, cols = gradients.shape
    rank = old_basis.shape[2]
    any_space = pl.BlockSpec(memory_space=pl.ANY)
    vmem = pl.BlockSpec(memory_space=pltpu.VMEM)
    f32 = jnp.float32
    stage = [
        pltpu.VMEM((matrices, HALF * NY, 8, 128), f32),
        pltpu.VMEM((PLANE, 8, 128), f32),
        pltpu.VMEM((8, 128), f32),
        pltpu.VMEM((NZ, 8, 128), f32),
        pltpu.VMEM((8, 128), f32),
        pltpu.VMEM((matrices, HALF * NY, 8, 128), f32),
    ]
    merged, factors, basis = pl.pallas_call(
        reduce_kernel,
        out_shape=(
            pltpu.VMEM((matrices, rows, cols), f32),
            pltpu.VMEM((matrices, rows, 128), jnp.bfloat16),
            pltpu.VMEM((matrices, rank, cols), f32),
        ),
        in_specs=[pl.BlockSpec(memory_space=pltpu.HBM)] * 3,
        out_specs=(vmem,) * 3,
        scratch_shapes=[
            pltpu.VMEM((matrices, rows, cols), jnp.bfloat16),
            pltpu.VMEM((matrices, rows, cols), jnp.bfloat16),
            pltpu.VMEM((matrices, rank, cols), f32),
        ]
        + stage
        + stage
        + [
            pltpu.SemaphoreType.DMA((matrices, rows // LOAD, 2)),
            pltpu.SemaphoreType.DMA,
            pltpu.SemaphoreType.DMA((8,)),
            pltpu.SemaphoreType.DMA((8,)),
        ],
        compiler_params=pltpu.CompilerParams(
            collective_id=0, has_side_effects=True, vmem_limit_bytes=50 << 20
        ),
        name="reduce",
    )(gradients[0, 0], errors[0, 0], jnp.swapaxes(old_basis, 1, 2))
    residual, new_basis = pl.pallas_call(
        residual_kernel,
        out_shape=(
            jax.ShapeDtypeStruct((matrices, rows, cols), jnp.bfloat16),
            jax.ShapeDtypeStruct((matrices, rank, cols), f32),
        ),
        in_specs=[vmem] * 3,
        out_specs=(any_space,) * 2,
        scratch_shapes=[
            pltpu.VMEM((matrices, rows, cols), jnp.bfloat16),
            pltpu.SemaphoreType.DMA,
            pltpu.SemaphoreType.DMA,
        ],
        compiler_params=pltpu.CompilerParams(vmem_limit_bytes=24 << 20),
        name="residual",
    )(merged, factors, basis)
    return residual[None, None], jnp.swapaxes(new_basis, 1, 2)


def solution(mesh):
    in_specs = (P("dp", "outer", None, None, None), P("dp", "outer", None, None, None), P())
    out_specs = (P("dp", "outer", None, None, None), P())
    return jax.shard_map(shards, mesh=mesh, in_specs=in_specs, out_specs=out_specs, check_vma=False)
```

```python
import functools
import itertools

import jax
import jax.numpy as jnp
from jax import lax
from jax.experimental import pallas as pl
from jax.experimental.pallas import tpu as pltpu
from jax.sharding import PartitionSpec as P

MESH = pl.DeviceIdType.MESH
HIGHEST = lax.Precision.HIGHEST
EPSILON = 1e-06
NX, NY, NZ, NC = 4, 4, 8, 2
PLANE = NX * NY * NC
REPLICAS = PLANE * NZ
BLOCK = 256
LOAD = 512
OUT = 128
HALF, FIRST, SECOND = 2, 2, 0


def ring(d, n):
    return min(d % n, n - d % n)


XY_OFFSETS = sorted(itertools.product(range(NX), range(NY)), key=lambda o: -(ring(o[0], NX) + ring(o[1], NY)))
Z_OFFSETS = sorted(range(1, NZ), key=lambda d: -ring(d, NZ))


def split3(value):
    high = value.astype(jnp.bfloat16).astype(jnp.float32)
    rest = value - high
    middle = rest.astype(jnp.bfloat16).astype(jnp.float32)
    return high, middle, rest - middle


def stacked(value):
    return jnp.concatenate(split3(value), axis=0).astype(jnp.bfloat16)


def tree_sum(terms):
    while len(terms) > 1:
        terms = [a + b for a, b in zip(terms[::2], terms[1::2])]
    return terms[0]


def fold(product):
    return product[0:8] + product[8:16] + product[16:24]


def reduce_kernel(
    g_hbm, e_hbm, q_hbm,
    merged, factors, basis,
    gv, ev, qv, send1, slot1, part1, zslot1, final1, gather1,
    send2, slot2, part2, zslot2, final2, gather2,
    in_sem, q_sem, send_sem, recv_sem,
):
    _, rows, cols = gv.shape
    per = rows // LOAD
    dp, y = lax.axis_index("dp"), lax.axis_index("outer")
    x, z, c = lax.div(dp, NZ * NC), lax.rem(lax.div(dp, NC), NZ), lax.rem(dp, NC)
    own, other = c, 1 - c
    sender = (x * NY + y) * NC + c
    half, column_of_half = lax.div(x, HALF), lax.rem(x, HALF)
    mine = column_of_half * NY + y

    q_copy = pltpu.make_async_copy(q_hbm, qv, q_sem)
    q_copy.start()
    loads = []
    for n, m in enumerate((other, own)):
        for i in range(per):
            at = pl.ds(i * LOAD, LOAD)
            pair = []
            for a, (src, dst) in enumerate(((g_hbm, gv), (e_hbm, ev))):
                copy = pltpu.make_async_copy(src.at[m, at], dst.at[m, at], in_sem.at[n, i, a])
                copy.start(priority=1)
                pair.append(copy)
            loads.append((n, m, i, pair))

    here, across = [], []
    for dx, dy in XY_OFFSETS:
        tx, ty = lax.rem(x + dx, NX), lax.rem(y + dy, NY)
        if dx or dy:
            here.append({"dp": (tx * NZ + z) * NC + own, "outer": ty})
        across.append({"dp": (tx * NZ + z) * NC + other, "outer": ty})
    column = [{"dp": (x * NZ + lax.rem(z + d, NZ)) * NC + c, "outer": y} for d in Z_OFFSETS]
    partners = across[:4] + column[:3] + here + across[4:] + column[3:]
    barrier = pltpu.get_barrier_semaphore()
    for device in partners:
        pl.semaphore_signal(barrier, inc=1, device_id=device, device_id_type=MESH)

    def wait_all(ref, sem):
        pltpu.make_async_copy(ref, ref, sem).wait()

    def remote(src, dst, send, recv, device):
        pltpu.make_async_remote_copy(
            src_ref=src, dst_ref=dst, send_sem=send_sem.at[send], recv_sem=recv_sem.at[recv],
            device_id=device, device_id_type=MESH,
        ).start()

    def targets(core, first):
        for dy in (2, 1, 3, 0):
            for i in range(HALF):
                ty = lax.rem(y + dy, NY)
                yield dy, i, i * NY + ty, {"dp": ((first + i) * NZ + z) * NC + core, "outer": ty}

    def scatter_across(send, m, slot, k, first):
        for _, _, index, device in targets(other, first):
            remote(send.at[m, index], slot.at[sender], k, k, device)

    def scatter_here(send, m, slot, k, first):
        for dy, i, index, device in targets(own, first):
            if dy:
                remote(send.at[m, index], slot.at[sender], k, k, device)
                continue

            @pl.when(x == first + i)
            def _():
                pltpu.make_async_copy(send.at[m, index], slot.at[sender], recv_sem.at[k]).start()

            @pl.when(x != first + i)
            def _():
                remote(send.at[m, index], slot.at[sender], k, k, device)

    def exchange(slot, part, zslot, k):
        wait_all(slot, recv_sem.at[k])
        part[...] = tree_sum([slot[i] for i in range(PLANE)])
        for device in column:
            remote(part, zslot.at[z], k + 1, k + 1, device)
        pltpu.make_async_copy(part, zslot.at[z], recv_sem.at[k + 1]).start()

    def spread(zslot, final, gather, m, k):
        wait_all(zslot, recv_sem.at[k + 1])
        final[...] = tree_sum([zslot[i] for i in range(NZ)]) * (1.0 / REPLICAS)
        for device in here:
            remote(final, gather.at[m, mine], k + 2, k + 2, device)
        for device in across:
            remote(final, gather.at[m, mine], k + 2, k + 3, device)
        pltpu.make_async_copy(final, gather.at[m, mine], recv_sem.at[k + 2]).start()

    def assembled(gather, m, blocks):
        return jnp.concatenate([gather[m, b] for b in range(blocks)], axis=1)

    def place(send, m, b, tile):
        send[m, b] = tile

    contract_last = (((1,), (1,)), ((), ()))
    q_copy.wait()
    q_terms = [stacked(qv[m]) for m in (other, own)]
    for n, m, i, pair in loads:
        for copy in pair:
            copy.wait()
        at = pl.ds(i * LOAD, LOAD)
        left = fold(
            lax.dot_general(q_terms[n], gv[m, at], contract_last, preferred_element_type=jnp.float32)
            + lax.dot_general(q_terms[n], ev[m, at], contract_last, preferred_element_type=jnp.float32)
        )
        for b in range(LOAD // 128):
            place(send1, m, i * (LOAD // 128) + b, left[:, b * 128 : (b + 1) * 128])
    pl.semaphore_wait(barrier, len(partners))
    scatter_across(send1, other, slot1, 0, FIRST)
    scatter_here(send1, own, slot1, 0, FIRST)
    for n in range(2):
        for i in range(rows // BLOCK):
            at = pl.ds(i * BLOCK, BLOCK)
            merged[n, at] = gv[n, at].astype(jnp.float32) + ev[n, at].astype(jnp.float32)

    @pl.when(half == FIRST // HALF)
    def _():
        exchange(slot1, part1, zslot1, 0)
        spread(zslot1, final1, gather1, own, 0)


    def right(m):
        mean = assembled(gather1, m, rows // 128)
        terms = stacked(mean)
        product = fold(
            jnp.dot(terms, gv[m], preferred_element_type=jnp.float32)
            + jnp.dot(terms, ev[m], preferred_element_type=jnp.float32)
        )
        for b in range(cols // 128):
            place(send2, m, b, product[:, b * 128 : (b + 1) * 128])
        for b in range(cols // 128, 8):
            place(send2, m, b, jnp.zeros((8, 128), jnp.float32))
        return mean

    wait_all(gather1.at[own], recv_sem.at[2])
    wait_all(gather1.at[other], recv_sem.at[3])
    mean_own = right(own)
    mean_other = right(other)
    scatter_across(send2, own, slot2, 4, SECOND)
    scatter_here(send2, other, slot2, 4, SECOND)

    row_of = lax.broadcasted_iota(jnp.int32, (8, 1), 0)
    eye = (
        lax.broadcasted_iota(jnp.int32, (8, 8), 0) == lax.broadcasted_iota(jnp.int32, (8, 8), 1)
    ).astype(jnp.float32)
    solutions = []
    for m, mean in ((own, mean_own), (other, mean_other)):
        gram = lax.dot_general(mean, mean, contract_last, precision=HIGHEST, preferred_element_type=jnp.float32)
        gram = gram + EPSILON * eye
        inverse, solved = eye, mean
        for k in range(8):
            pivot = jnp.sqrt(gram[k : k + 1, k : k + 1])
            across_row = gram[k : k + 1, :] / pivot
            below = jnp.where(row_of > k, gram[:, k : k + 1] / pivot, 0.0)
            gram = gram - below * across_row
            first = inverse[k : k + 1, :] / pivot
            inverse = jnp.where(row_of == k, first, inverse - below * first)
            first = solved[k : k + 1, :] / pivot
            solved = jnp.where(row_of == k, first, solved - below * first)
        solutions.append((m, inverse, solved))

    @pl.when(half == SECOND // HALF)
    def _():
        exchange(slot2, part2, zslot2, 4)

    for m, _, solved in solutions:
        o1, o2, o3 = split3(solved)
        wide = jnp.concatenate([o1, o1, o2, o2, o1, o3, jnp.zeros((80, rows), jnp.float32)], axis=0)
        factors[m] = jnp.transpose(wide).astype(jnp.bfloat16)

    @pl.when(half == SECOND // HALF)
    def _():
        spread(zslot2, final2, gather2, other, 4)

    wait_all(gather2.at[other], recv_sem.at[6])
    wait_all(gather2.at[own], recv_sem.at[7])
    for m, inverse, _ in solutions:
        raw = assembled(gather2, m, cols // 128)
        basis[m] = tree_sum([inverse[:, t : t + 1] * raw[t : t + 1, :] for t in range(8)])

    for k, first in ((0, FIRST), (4, SECOND)):

        @pl.when(half == first // HALF)
        def _():
            wait_all(slot1.at[pl.ds(0, NC * HALF * NY - 1)], send_sem.at[k])
            wait_all(zslot1.at[pl.ds(0, NZ - 1)], send_sem.at[k + 1])
            wait_all(slot1.at[pl.ds(0, PLANE - 1)], send_sem.at[k + 2])

        @pl.when(half != first // HALF)
        def _():
            wait_all(slot1.at[pl.ds(0, NC * HALF * NY)], send_sem.at[k])


def residual_kernel(merged, factors, basis, out_hbm, basis_hbm, buffer, out_sem, basis_sem):
    matrices, rows, cols = merged.shape
    basis_copy = pltpu.make_async_copy(basis, basis_hbm, basis_sem)
    basis_copy.start()
    for m in range(matrices):
        b1, b2, b3 = split3(basis[m])
        terms = jnp.concatenate(
            [b1, b2, b1, b2, b3, b1, jnp.zeros((80, cols), jnp.float32)], axis=0
        ).astype(jnp.bfloat16)
        for i in range(rows // OUT):
            at = pl.ds(i * OUT, OUT)
            update = jnp.dot(factors[m, at], terms, preferred_element_type=jnp.float32)
            buffer[m, at] = (merged[m, at] - update).astype(jnp.bfloat16)
            pltpu.make_async_copy(buffer.at[m, at], out_hbm.at[m, at], out_sem).start(priority=i % 2)
    pltpu.make_async_copy(buffer, out_hbm, out_sem).wait()
    basis_copy.wait()


def shards(gradients, errors, old_basis):
    _, _, matrices, rows, cols = gradients.shape
    rank = old_basis.shape[2]
    any_space = pl.BlockSpec(memory_space=pl.ANY)
    vmem = pl.BlockSpec(memory_space=pltpu.VMEM)
    f32 = jnp.float32
    stage = [
        pltpu.VMEM((matrices, HALF * NY, 8, 128), f32),
        pltpu.VMEM((PLANE, 8, 128), f32),
        pltpu.VMEM((8, 128), f32),
        pltpu.VMEM((NZ, 8, 128), f32),
        pltpu.VMEM((8, 128), f32),
        pltpu.VMEM((matrices, HALF * NY, 8, 128), f32),
    ]
    merged, factors, basis = pl.pallas_call(
        reduce_kernel,
        out_shape=(
            pltpu.VMEM((matrices, rows, cols), f32),
            pltpu.VMEM((matrices, rows, 128), jnp.bfloat16),
            pltpu.VMEM((matrices, rank, cols), f32),
        ),
        in_specs=[pl.BlockSpec(memory_space=pltpu.HBM)] * 3,
        out_specs=(vmem,) * 3,
        scratch_shapes=[
            pltpu.VMEM((matrices, rows, cols), jnp.bfloat16),
            pltpu.VMEM((matrices, rows, cols), jnp.bfloat16),
            pltpu.VMEM((matrices, rank, cols), f32),
        ]
        + stage
        + stage
        + [
            pltpu.SemaphoreType.DMA((matrices, rows // LOAD, 2)),
            pltpu.SemaphoreType.DMA,
            pltpu.SemaphoreType.DMA((8,)),
            pltpu.SemaphoreType.DMA((8,)),
        ],
        compiler_params=pltpu.CompilerParams(
            collective_id=0, has_side_effects=True, vmem_limit_bytes=50 << 20
        ),
        name="reduce",
    )(gradients[0, 0], errors[0, 0], jnp.swapaxes(old_basis, 1, 2))
    residual, new_basis = pl.pallas_call(
        residual_kernel,
        out_shape=(
            jax.ShapeDtypeStruct((matrices, rows, cols), jnp.bfloat16),
            jax.ShapeDtypeStruct((matrices, rank, cols), f32),
        ),
        in_specs=[vmem] * 3,
        out_specs=(any_space,) * 2,
        scratch_shapes=[
            pltpu.VMEM((matrices, rows, cols), jnp.bfloat16),
            pltpu.SemaphoreType.DMA,
            pltpu.SemaphoreType.DMA,
        ],
        compiler_params=pltpu.CompilerParams(vmem_limit_bytes=24 << 20),
        name="residual",
    )(merged, factors, basis)
    return residual[None, None], jnp.swapaxes(new_basis, 1, 2)


def solution(mesh):
    in_specs = (P("dp", "outer", None, None, None), P("dp", "outer", None, None, None), P())
    out_specs = (P("dp", "outer", None, None, None), P())
    return jax.shard_map(shards, mesh=mesh, in_specs=in_specs, out_specs=out_specs, check_vma=False)
```

```python
import functools
import itertools

import jax
import jax.numpy as jnp
from jax import lax
from jax.experimental import pallas as pl
from jax.experimental.pallas import tpu as pltpu
from jax.sharding import PartitionSpec as P

MESH = pl.DeviceIdType.MESH
HIGHEST = lax.Precision.HIGHEST
EPSILON = 1e-06
NX, NY, NZ, NC = 4, 4, 8, 2
PLANE = NX * NY * NC
REPLICAS = PLANE * NZ
BLOCK = 256
LOAD = 512
OUT = 128
HALF, FIRST, SECOND = 2, 2, 0


def ring(d, n):
    return min(d % n, n - d % n)


XY_OFFSETS = sorted(itertools.product(range(NX), range(NY)), key=lambda o: -(ring(o[0], NX) + ring(o[1], NY)))
Z_OFFSETS = sorted(range(1, NZ), key=lambda d: -ring(d, NZ))


def split3(value):
    high = value.astype(jnp.bfloat16).astype(jnp.float32)
    rest = value - high
    middle = rest.astype(jnp.bfloat16).astype(jnp.float32)
    return high, middle, rest - middle


def stacked(value):
    return jnp.concatenate(split3(value), axis=0).astype(jnp.bfloat16)


def tree_sum(terms):
    while len(terms) > 1:
        terms = [a + b for a, b in zip(terms[::2], terms[1::2])]
    return terms[0]


def fold(product):
    return product[0:8] + product[8:16] + product[16:24]


def reduce_kernel(
    g_hbm, e_hbm, q_hbm,
    merged, factors, basis,
    gv, ev, qv, send1, slot1, part1, zslot1, final1, gather1,
    send2, slot2, part2, zslot2, final2, gather2,
    in_sem, q_sem, send_sem, recv_sem,
):
    _, rows, cols = gv.shape
    per = rows // LOAD
    dp, y = lax.axis_index("dp"), lax.axis_index("outer")
    x, z, c = lax.div(dp, NZ * NC), lax.rem(lax.div(dp, NC), NZ), lax.rem(dp, NC)
    own, other = c, 1 - c
    sender = (x * NY + y) * NC + c
    half, column_of_half = lax.div(x, HALF), lax.rem(x, HALF)
    mine = column_of_half * NY + y

    q_copy = pltpu.make_async_copy(q_hbm, qv, q_sem)
    q_copy.start()
    loads = []
    for n, m in enumerate((other, own)):
        for i in range(per):
            at = pl.ds(i * LOAD, LOAD)
            pair = []
            for a, (src, dst) in enumerate(((g_hbm, gv), (e_hbm, ev))):
                copy = pltpu.make_async_copy(src.at[m, at], dst.at[m, at], in_sem.at[n, i, a])
                copy.start(priority=1)
                pair.append(copy)
            loads.append((n, m, i, pair))

    here, across = [], []
    for dx, dy in XY_OFFSETS:
        tx, ty = lax.rem(x + dx, NX), lax.rem(y + dy, NY)
        if dx or dy:
            here.append({"dp": (tx * NZ + z) * NC + own, "outer": ty})
        across.append({"dp": (tx * NZ + z) * NC + other, "outer": ty})
    column = [{"dp": (x * NZ + lax.rem(z + d, NZ)) * NC + c, "outer": y} for d in Z_OFFSETS]
    partners = across[:4] + column[:3] + here + across[4:] + column[3:]
    barrier = pltpu.get_barrier_semaphore()
    for device in partners:
        pl.semaphore_signal(barrier, inc=1, device_id=device, device_id_type=MESH)

    def wait_all(ref, sem):
        pltpu.make_async_copy(ref, ref, sem).wait()

    def remote(src, dst, send, recv, device):
        pltpu.make_async_remote_copy(
            src_ref=src, dst_ref=dst, send_sem=send_sem.at[send], recv_sem=recv_sem.at[recv],
            device_id=device, device_id_type=MESH,
        ).start()

    def targets(core, first):
        for dy in (2, 1, 3, 0):
            for i in range(HALF):
                ty = lax.rem(y + dy, NY)
                yield dy, i, i * NY + ty, {"dp": ((first + i) * NZ + z) * NC + core, "outer": ty}

    def scatter_across(send, m, slot, k, first):
        for _, _, index, device in targets(other, first):
            remote(send.at[m, index], slot.at[sender], k, k, device)

    def scatter_here(send, m, slot, k, first):
        for dy, i, index, device in targets(own, first):
            if dy:
                remote(send.at[m, index], slot.at[sender], k, k, device)
                continue

            @pl.when(x == first + i)
            def _():
                pltpu.make_async_copy(send.at[m, index], slot.at[sender], recv_sem.at[k]).start()

            @pl.when(x != first + i)
            def _():
                remote(send.at[m, index], slot.at[sender], k, k, device)

    def exchange(slot, part, zslot, k):
        wait_all(slot, recv_sem.at[k])
        part[...] = tree_sum([slot[i] for i in range(PLANE)])
        for device in column:
            remote(part, zslot.at[z], k + 1, k + 1, device)
        pltpu.make_async_copy(part, zslot.at[z], recv_sem.at[k + 1]).start()

    def spread(zslot, final, gather, m, k):
        wait_all(zslot, recv_sem.at[k + 1])
        final[...] = tree_sum([zslot[i] for i in range(NZ)]) * (1.0 / REPLICAS)
        for device in here:
            remote(final, gather.at[m, mine], k + 2, k + 2, device)
        for device in across:
            remote(final, gather.at[m, mine], k + 2, k + 3, device)
        pltpu.make_async_copy(final, gather.at[m, mine], recv_sem.at[k + 2]).start()

    def assembled(gather, m, blocks):
        return jnp.concatenate([gather[m, b] for b in range(blocks)], axis=1)

    def place(send, m, b, tile):
        send[m, b] = tile

    contract_last = (((1,), (1,)), ((), ()))
    q_copy.wait()
    q_terms = [stacked(qv[m]) for m in (other, own)]
    for n, m, i, pair in loads:
        for copy in pair:
            copy.wait()
        at = pl.ds(i * LOAD, LOAD)
        left = fold(
            lax.dot_general(q_terms[n], gv[m, at], contract_last, preferred_element_type=jnp.float32)
            + lax.dot_general(q_terms[n], ev[m, at], contract_last, preferred_element_type=jnp.float32)
        )
        for b in range(LOAD // 128):
            place(send1, m, i * (LOAD // 128) + b, left[:, b * 128 : (b + 1) * 128])
    pl.semaphore_wait(barrier, len(partners))
    scatter_across(send1, other, slot1, 0, FIRST)
    scatter_here(send1, own, slot1, 0, FIRST)
    for n in range(2):
        for i in range(rows // BLOCK):
            at = pl.ds(i * BLOCK, BLOCK)
            merged[n, at] = gv[n, at].astype(jnp.float32) + ev[n, at].astype(jnp.float32)

    @pl.when(half == FIRST // HALF)
    def _():
        exchange(slot1, part1, zslot1, 0)
        spread(zslot1, final1, gather1, own, 0)


    def right(m):
        mean = assembled(gather1, m, rows // 128)
        terms = stacked(mean)
        product = fold(
            jnp.dot(terms, gv[m], preferred_element_type=jnp.float32)
            + jnp.dot(terms, ev[m], preferred_element_type=jnp.float32)
        )
        for b in range(cols // 128):
            place(send2, m, b, product[:, b * 128 : (b + 1) * 128])
        for b in range(cols // 128, 8):
            place(send2, m, b, jnp.zeros((8, 128), jnp.float32))
        return mean

    wait_all(gather1.at[own], recv_sem.at[2])
    wait_all(gather1.at[other], recv_sem.at[3])
    mean_own = right(own)
    mean_other = right(other)
    scatter_across(send2, own, slot2, 4, SECOND)
    scatter_here(send2, other, slot2, 4, SECOND)

    row_of = lax.broadcasted_iota(jnp.int32, (8, 1), 0)
    eye = (
        lax.broadcasted_iota(jnp.int32, (8, 8), 0) == lax.broadcasted_iota(jnp.int32, (8, 8), 1)
    ).astype(jnp.float32)
    solutions = []
    for m, mean in ((own, mean_own), (other, mean_other)):
        gram = lax.dot_general(mean, mean, contract_last, precision=HIGHEST, preferred_element_type=jnp.float32)
        gram = gram + EPSILON * eye
        inverse, solved = eye, mean
        for k in range(8):
            pivot = jnp.sqrt(gram[k : k + 1, k : k + 1])
            across_row = gram[k : k + 1, :] / pivot
            below = jnp.where(row_of > k, gram[:, k : k + 1] / pivot, 0.0)
            gram = gram - below * across_row
            first = inverse[k : k + 1, :] / pivot
            inverse = jnp.where(row_of == k, first, inverse - below * first)
            first = solved[k : k + 1, :] / pivot
            solved = jnp.where(row_of == k, first, solved - below * first)
        solutions.append((m, inverse, solved))

    @pl.when(half == SECOND // HALF)
    def _():
        exchange(slot2, part2, zslot2, 4)

    for m, _, solved in solutions:
        o1, o2, o3 = split3(solved)
        wide = jnp.concatenate([o1, o1, o2, o2, o1, o3, jnp.zeros((80, rows), jnp.float32)], axis=0)
        factors[m] = jnp.transpose(wide).astype(jnp.bfloat16)

    @pl.when(half == SECOND // HALF)
    def _():
        spread(zslot2, final2, gather2, other, 4)

    for (m, inverse, _), group in ((solutions[1], 6), (solutions[0], 7)):
        wait_all(gather2.at[m], recv_sem.at[group])
        raw = assembled(gather2, m, cols // 128)
        basis[m] = tree_sum([inverse[:, t : t + 1] * raw[t : t + 1, :] for t in range(8)])

    for k, first in ((0, FIRST), (4, SECOND)):

        @pl.when(half == first // HALF)
        def _():
            wait_all(slot1.at[pl.ds(0, NC * HALF * NY - 1)], send_sem.at[k])
            wait_all(zslot1.at[pl.ds(0, NZ - 1)], send_sem.at[k + 1])
            wait_all(slot1.at[pl.ds(0, PLANE - 1)], send_sem.at[k + 2])

        @pl.when(half != first // HALF)
        def _():
            wait_all(slot1.at[pl.ds(0, NC * HALF * NY)], send_sem.at[k])


def residual_kernel(merged, factors, basis, out_hbm, basis_hbm, buffer, out_sem, basis_sem):
    matrices, rows, cols = merged.shape
    basis_copy = pltpu.make_async_copy(basis, basis_hbm, basis_sem)
    basis_copy.start()
    for m in range(matrices):
        b1, b2, b3 = split3(basis[m])
        terms = jnp.concatenate(
            [b1, b2, b1, b2, b3, b1, jnp.zeros((80, cols), jnp.float32)], axis=0
        ).astype(jnp.bfloat16)
        for i in range(rows // OUT):
            at = pl.ds(i * OUT, OUT)
            update = jnp.dot(factors[m, at], terms, preferred_element_type=jnp.float32)
            buffer[m, at] = (merged[m, at] - update).astype(jnp.bfloat16)
            pltpu.make_async_copy(buffer.at[m, at], out_hbm.at[m, at], out_sem).start(priority=i % 2)
    pltpu.make_async_copy(buffer, out_hbm, out_sem).wait()
    basis_copy.wait()


def shards(gradients, errors, old_basis):
    _, _, matrices, rows, cols = gradients.shape
    rank = old_basis.shape[2]
    any_space = pl.BlockSpec(memory_space=pl.ANY)
    vmem = pl.BlockSpec(memory_space=pltpu.VMEM)
    f32 = jnp.float32
    stage = [
        pltpu.VMEM((matrices, HALF * NY, 8, 128), f32),
        pltpu.VMEM((PLANE, 8, 128), f32),
        pltpu.VMEM((8, 128), f32),
        pltpu.VMEM((NZ, 8, 128), f32),
        pltpu.VMEM((8, 128), f32),
        pltpu.VMEM((matrices, HALF * NY, 8, 128), f32),
    ]
    merged, factors, basis = pl.pallas_call(
        reduce_kernel,
        out_shape=(
            pltpu.VMEM((matrices, rows, cols), f32),
            pltpu.VMEM((matrices, rows, 128), jnp.bfloat16),
            pltpu.VMEM((matrices, rank, cols), f32),
        ),
        in_specs=[pl.BlockSpec(memory_space=pltpu.HBM)] * 3,
        out_specs=(vmem,) * 3,
        scratch_shapes=[
            pltpu.VMEM((matrices, rows, cols), jnp.bfloat16),
            pltpu.VMEM((matrices, rows, cols), jnp.bfloat16),
            pltpu.VMEM((matrices, rank, cols), f32),
        ]
        + stage
        + stage
        + [
            pltpu.SemaphoreType.DMA((matrices, rows // LOAD, 2)),
            pltpu.SemaphoreType.DMA,
            pltpu.SemaphoreType.DMA((8,)),
            pltpu.SemaphoreType.DMA((8,)),
        ],
        compiler_params=pltpu.CompilerParams(
            collective_id=0, has_side_effects=True, vmem_limit_bytes=50 << 20
        ),
        name="reduce",
    )(gradients[0, 0], errors[0, 0], jnp.swapaxes(old_basis, 1, 2))
    residual, new_basis = pl.pallas_call(
        residual_kernel,
        out_shape=(
            jax.ShapeDtypeStruct((matrices, rows, cols), jnp.bfloat16),
            jax.ShapeDtypeStruct((matrices, rank, cols), f32),
        ),
        in_specs=[vmem] * 3,
        out_specs=(any_space,) * 2,
        scratch_shapes=[
            pltpu.VMEM((matrices, rows, cols), jnp.bfloat16),
            pltpu.SemaphoreType.DMA,
            pltpu.SemaphoreType.DMA,
        ],
        compiler_params=pltpu.CompilerParams(vmem_limit_bytes=24 << 20),
        name="residual",
    )(merged, factors, basis)
    return residual[None, None], jnp.swapaxes(new_basis, 1, 2)


def solution(mesh):
    in_specs = (P("dp", "outer", None, None, None), P("dp", "outer", None, None, None), P())
    out_specs = (P("dp", "outer", None, None, None), P())
    return jax.shard_map(shards, mesh=mesh, in_specs=in_specs, out_specs=out_specs, check_vma=False)
```

```python
import functools
import itertools

import jax
import jax.numpy as jnp
from jax import lax
from jax.experimental import pallas as pl
from jax.experimental.pallas import tpu as pltpu
from jax.sharding import PartitionSpec as P

MESH = pl.DeviceIdType.MESH
HIGHEST = lax.Precision.HIGHEST
EPSILON = 1e-06
NX, NY, NZ, NC = 4, 4, 8, 2
PLANE = NX * NY * NC
REPLICAS = PLANE * NZ
BLOCK = 256
LOAD = 512
OUT = 128
HALF, FIRST, SECOND = 2, 2, 0


def ring(d, n):
    return min(d % n, n - d % n)


XY_OFFSETS = sorted(itertools.product(range(NX), range(NY)), key=lambda o: -(ring(o[0], NX) + ring(o[1], NY)))
Z_OFFSETS = sorted(range(1, NZ), key=lambda d: -ring(d, NZ))


def split3(value):
    high = value.astype(jnp.bfloat16).astype(jnp.float32)
    rest = value - high
    middle = rest.astype(jnp.bfloat16).astype(jnp.float32)
    return high, middle, rest - middle


def stacked(value):
    return jnp.concatenate(split3(value), axis=0).astype(jnp.bfloat16)


def tree_sum(terms):
    while len(terms) > 1:
        terms = [a + b for a, b in zip(terms[::2], terms[1::2])]
    return terms[0]


def fold(product):
    return product[0:8] + product[8:16] + product[16:24]


def reduce_kernel(
    g_hbm, e_hbm, q_hbm,
    merged, factors, basis,
    gv, ev, qv, send1, slot1, part1, zslot1, final1, gather1,
    send2, slot2, part2, zslot2, final2, gather2,
    in_sem, q_sem, send_sem, recv_sem,
):
    _, rows, cols = gv.shape
    per = rows // LOAD
    dp, y = lax.axis_index("dp"), lax.axis_index("outer")
    x, z, c = lax.div(dp, NZ * NC), lax.rem(lax.div(dp, NC), NZ), lax.rem(dp, NC)
    own, other = c, 1 - c
    sender = (x * NY + y) * NC + c
    half, column_of_half = lax.div(x, HALF), lax.rem(x, HALF)
    mine = column_of_half * NY + y

    q_copy = pltpu.make_async_copy(q_hbm, qv, q_sem)
    q_copy.start()
    loads = []
    for n, m in enumerate((other, own)):
        for i in range(per):
            at = pl.ds(i * LOAD, LOAD)
            pair = []
            for a, (src, dst) in enumerate(((g_hbm, gv), (e_hbm, ev))):
                copy = pltpu.make_async_copy(src.at[m, at], dst.at[m, at], in_sem.at[n, i, a])
                copy.start(priority=1)
                pair.append(copy)
            loads.append((n, m, i, pair))

    here, across = [], []
    for dx, dy in XY_OFFSETS:
        tx, ty = lax.rem(x + dx, NX), lax.rem(y + dy, NY)
        if dx or dy:
            here.append({"dp": (tx * NZ + z) * NC + own, "outer": ty})
        across.append({"dp": (tx * NZ + z) * NC + other, "outer": ty})
    column = [{"dp": (x * NZ + lax.rem(z + d, NZ)) * NC + c, "outer": y} for d in Z_OFFSETS]
    partners = across[:4] + column[:3] + here + across[4:] + column[3:]
    barrier = pltpu.get_barrier_semaphore()
    for device in partners:
        pl.semaphore_signal(barrier, inc=1, device_id=device, device_id_type=MESH)

    def wait_all(ref, sem):
        pltpu.make_async_copy(ref, ref, sem).wait()

    def remote(src, dst, send, recv, device):
        pltpu.make_async_remote_copy(
            src_ref=src, dst_ref=dst, send_sem=send_sem.at[send], recv_sem=recv_sem.at[recv],
            device_id=device, device_id_type=MESH,
        ).start()

    def targets(core, first):
        for dy in (2, 1, 3, 0):
            for i in range(HALF):
                ty = lax.rem(y + dy, NY)
                yield dy, i, i * NY + ty, {"dp": ((first + i) * NZ + z) * NC + core, "outer": ty}

    def scatter_across(send, m, slot, k, first):
        for _, _, index, device in targets(other, first):
            remote(send.at[m, index], slot.at[sender], k, k, device)

    def scatter_here(send, m, slot, k, first):
        for dy, i, index, device in targets(own, first):
            if dy:
                remote(send.at[m, index], slot.at[sender], k, k, device)
                continue

            @pl.when(x == first + i)
            def _():
                pltpu.make_async_copy(send.at[m, index], slot.at[sender], recv_sem.at[k]).start()

            @pl.when(x != first + i)
            def _():
                remote(send.at[m, index], slot.at[sender], k, k, device)

    def exchange(slot, part, zslot, k):
        wait_all(slot, recv_sem.at[k])
        part[...] = tree_sum([slot[i] for i in range(PLANE)])
        for device in column:
            remote(part, zslot.at[z], k + 1, k + 1, device)
        pltpu.make_async_copy(part, zslot.at[z], recv_sem.at[k + 1]).start()

    def spread(zslot, final, gather, m, k):
        wait_all(zslot, recv_sem.at[k + 1])
        final[...] = tree_sum([zslot[i] for i in range(NZ)]) * (1.0 / REPLICAS)
        for device in here:
            remote(final, gather.at[m, mine], k + 2, k + 2, device)
        for device in across:
            remote(final, gather.at[m, mine], k + 2, k + 3, device)
        pltpu.make_async_copy(final, gather.at[m, mine], recv_sem.at[k + 2]).start()

    def assembled(gather, m, blocks):
        return jnp.concatenate([gather[m, b] for b in range(blocks)], axis=1)

    def place(send, m, b, tile):
        send[m, b] = tile

    contract_last = (((1,), (1,)), ((), ()))
    q_copy.wait()
    q_terms = []
    for m in (other, own):
        wide = jnp.concatenate([*split3(qv[m]), jnp.zeros((104, cols), jnp.float32)], axis=0)
        q_terms.append(jnp.transpose(wide).astype(jnp.bfloat16))

    def finish(m, i, product):
        left = fold(jnp.transpose(product))
        for b in range(LOAD // 128):
            place(send1, m, i * (LOAD // 128) + b, left[:, b * 128 : (b + 1) * 128])

    pending = None
    for n, m, i, pair in loads:
        for copy in pair:
            copy.wait()
        at = pl.ds(i * LOAD, LOAD)
        product = jnp.dot(gv[m, at], q_terms[n], preferred_element_type=jnp.float32) + jnp.dot(
            ev[m, at], q_terms[n], preferred_element_type=jnp.float32
        )
        if pending is not None:
            finish(*pending)
        pending = (m, i, product)
    finish(*pending)
    pl.semaphore_wait(barrier, len(partners))
    scatter_across(send1, other, slot1, 0, FIRST)
    scatter_here(send1, own, slot1, 0, FIRST)
    for n in range(2):
        for i in range(rows // BLOCK):
            at = pl.ds(i * BLOCK, BLOCK)
            merged[n, at] = gv[n, at].astype(jnp.float32) + ev[n, at].astype(jnp.float32)

    @pl.when(half == FIRST // HALF)
    def _():
        exchange(slot1, part1, zslot1, 0)
        spread(zslot1, final1, gather1, own, 0)


    def right(m):
        mean = assembled(gather1, m, rows // 128)
        terms = stacked(mean)
        product = fold(
            jnp.dot(terms, gv[m], preferred_element_type=jnp.float32)
            + jnp.dot(terms, ev[m], preferred_element_type=jnp.float32)
        )
        for b in range(cols // 128):
            place(send2, m, b, product[:, b * 128 : (b + 1) * 128])
        for b in range(cols // 128, 8):
            place(send2, m, b, jnp.zeros((8, 128), jnp.float32))
        return mean

    wait_all(gather1.at[own], recv_sem.at[2])
    wait_all(gather1.at[other], recv_sem.at[3])
    mean_own = right(own)
    mean_other = right(other)
    scatter_across(send2, own, slot2, 4, SECOND)
    scatter_here(send2, other, slot2, 4, SECOND)

    row_of = lax.broadcasted_iota(jnp.int32, (8, 1), 0)
    eye = (
        lax.broadcasted_iota(jnp.int32, (8, 8), 0) == lax.broadcasted_iota(jnp.int32, (8, 8), 1)
    ).astype(jnp.float32)
    solutions = []
    for m, mean in ((own, mean_own), (other, mean_other)):
        gram = lax.dot_general(mean, mean, contract_last, precision=HIGHEST, preferred_element_type=jnp.float32)
        gram = gram + EPSILON * eye
        inverse, solved = eye, mean
        for k in range(8):
            pivot = jnp.sqrt(gram[k : k + 1, k : k + 1])
            across_row = gram[k : k + 1, :] / pivot
            below = jnp.where(row_of > k, gram[:, k : k + 1] / pivot, 0.0)
            gram = gram - below * across_row
            first = inverse[k : k + 1, :] / pivot
            inverse = jnp.where(row_of == k, first, inverse - below * first)
            first = solved[k : k + 1, :] / pivot
            solved = jnp.where(row_of == k, first, solved - below * first)
        solutions.append((m, inverse, solved))

    @pl.when(half == SECOND // HALF)
    def _():
        exchange(slot2, part2, zslot2, 4)

    for m, _, solved in solutions:
        o1, o2, o3 = split3(solved)
        wide = jnp.concatenate([o1, o1, o2, o2, o1, o3, jnp.zeros((80, rows), jnp.float32)], axis=0)
        factors[m] = jnp.transpose(wide).astype(jnp.bfloat16)

    @pl.when(half == SECOND // HALF)
    def _():
        spread(zslot2, final2, gather2, other, 4)

    for (m, inverse, _), group in ((solutions[1], 6), (solutions[0], 7)):
        wait_all(gather2.at[m], recv_sem.at[group])
        raw = assembled(gather2, m, cols // 128)
        basis[m] = tree_sum([inverse[:, t : t + 1] * raw[t : t + 1, :] for t in range(8)])

    for k, first in ((0, FIRST), (4, SECOND)):

        @pl.when(half == first // HALF)
        def _():
            wait_all(slot1.at[pl.ds(0, NC * HALF * NY - 1)], send_sem.at[k])
            wait_all(zslot1.at[pl.ds(0, NZ - 1)], send_sem.at[k + 1])
            wait_all(slot1.at[pl.ds(0, PLANE - 1)], send_sem.at[k + 2])

        @pl.when(half != first // HALF)
        def _():
            wait_all(slot1.at[pl.ds(0, NC * HALF * NY)], send_sem.at[k])


def residual_kernel(merged, factors, basis, out_hbm, basis_hbm, buffer, out_sem, basis_sem):
    matrices, rows, cols = merged.shape
    basis_copy = pltpu.make_async_copy(basis, basis_hbm, basis_sem)
    basis_copy.start()
    for m in range(matrices):
        b1, b2, b3 = split3(basis[m])
        terms = jnp.concatenate(
            [b1, b2, b1, b2, b3, b1, jnp.zeros((80, cols), jnp.float32)], axis=0
        ).astype(jnp.bfloat16)
        for i in range(rows // OUT):
            at = pl.ds(i * OUT, OUT)
            update = jnp.dot(factors[m, at], terms, preferred_element_type=jnp.float32)
            buffer[m, at] = (merged[m, at] - update).astype(jnp.bfloat16)
            pltpu.make_async_copy(buffer.at[m, at], out_hbm.at[m, at], out_sem).start(priority=i % 2)
    pltpu.make_async_copy(buffer, out_hbm, out_sem).wait()
    basis_copy.wait()


def shards(gradients, errors, old_basis):
    _, _, matrices, rows, cols = gradients.shape
    rank = old_basis.shape[2]
    any_space = pl.BlockSpec(memory_space=pl.ANY)
    vmem = pl.BlockSpec(memory_space=pltpu.VMEM)
    f32 = jnp.float32
    stage = [
        pltpu.VMEM((matrices, HALF * NY, 8, 128), f32),
        pltpu.VMEM((PLANE, 8, 128), f32),
        pltpu.VMEM((8, 128), f32),
        pltpu.VMEM((NZ, 8, 128), f32),
        pltpu.VMEM((8, 128), f32),
        pltpu.VMEM((matrices, HALF * NY, 8, 128), f32),
    ]
    merged, factors, basis = pl.pallas_call(
        reduce_kernel,
        out_shape=(
            pltpu.VMEM((matrices, rows, cols), f32),
            pltpu.VMEM((matrices, rows, 128), jnp.bfloat16),
            pltpu.VMEM((matrices, rank, cols), f32),
        ),
        in_specs=[pl.BlockSpec(memory_space=pltpu.HBM)] * 3,
        out_specs=(vmem,) * 3,
        scratch_shapes=[
            pltpu.VMEM((matrices, rows, cols), jnp.bfloat16),
            pltpu.VMEM((matrices, rows, cols), jnp.bfloat16),
            pltpu.VMEM((matrices, rank, cols), f32),
        ]
        + stage
        + stage
        + [
            pltpu.SemaphoreType.DMA((matrices, rows // LOAD, 2)),
            pltpu.SemaphoreType.DMA,
            pltpu.SemaphoreType.DMA((8,)),
            pltpu.SemaphoreType.DMA((8,)),
        ],
        compiler_params=pltpu.CompilerParams(
            collective_id=0, has_side_effects=True, vmem_limit_bytes=50 << 20
        ),
        name="reduce",
    )(gradients[0, 0], errors[0, 0], jnp.swapaxes(old_basis, 1, 2))
    residual, new_basis = pl.pallas_call(
        residual_kernel,
        out_shape=(
            jax.ShapeDtypeStruct((matrices, rows, cols), jnp.bfloat16),
            jax.ShapeDtypeStruct((matrices, rank, cols), f32),
        ),
        in_specs=[vmem] * 3,
        out_specs=(any_space,) * 2,
        scratch_shapes=[
            pltpu.VMEM((matrices, rows, cols), jnp.bfloat16),
            pltpu.SemaphoreType.DMA,
            pltpu.SemaphoreType.DMA,
        ],
        compiler_params=pltpu.CompilerParams(vmem_limit_bytes=24 << 20),
        name="residual",
    )(merged, factors, basis)
    return residual[None, None], jnp.swapaxes(new_basis, 1, 2)


def solution(mesh):
    in_specs = (P("dp", "outer", None, None, None), P("dp", "outer", None, None, None), P())
    out_specs = (P("dp", "outer", None, None, None), P())
    return jax.shard_map(shards, mesh=mesh, in_specs=in_specs, out_specs=out_specs, check_vma=False)
```
